32 devices in a mesh: groups: 2 (over y), tok: 4 (over z), dp: 2 (over x), head: 2 (over core).
Axes of the slice: x: 2, y: 2, z: 4, core: 2. Of those that a mesh axis runs over, the one named last changes fastest.
Arguments:
- features: bfloat16 [128, 4096], P(('groups', 'dp', 'head'), 'tok'), parts along dimension 0, may hold values from -6 to 6
- cross_down: bfloat16 [4096, 512], P('tok'), may hold values from -0.09375 to 0.09375
- cross_up: bfloat16 [512, 4096], P(None, 'tok'), may hold values from -0.25 to 0.25
- cross_bias: float32 [4096], P('tok'), may hold values from -4 to 4
- feature_token: int32 [4096], P('tok'), may hold values from 0 to 31, as said below
- proj_weight: bfloat16 [32, 128, 1536], P('tok'), may hold values from -0.5 to 0.5
- proj_bias: float32 [32, 1536], P('tok'), may hold values from -3 to 3
- mix_gain: float32 [32, 1536], P('tok'), may hold values from 0.1 to 1.9
- expand_weight: bfloat16 [32, 1536, 3072], P('tok', None, ('dp', 'head')), may hold values from -0.15625 to 0.15625
- expand_bias: float32 [32, 3072], P('tok', ('dp', 'head')), may hold values from -3 to 3
- contract_weight: bfloat16 [32, 3072, 1536], P('tok', ('dp', 'head')), may hold values from -0.109375 to 0.109375
- contract_bias: float32 [32, 1536], P('tok'), may hold values from -3 to 3
- block_gain: float32 [32, 1536], P('tok'), may hold values from 0.1 to 1.9
- gate_weight: bfloat16 [1536, 1536], P(None, ('dp', 'head')), may hold values from -0.15625 to 0.15625
- gate_bias: float32 [1536], replicated, may hold values from -4 to 4
Outputs:
- gated_states: bfloat16 [8, 16, 32, 1536], P(('groups', 'dp', 'head'), 'tok'), parts along dimension 0
The draws below stay inside these ranges and needn't reach their ends.
There are 2 independent parts, one for each index of `groups`. The reference program is written for one: setup_inputs(seed, part) draws one part's arguments, and reference() takes and returns one part's arrays. A program takes and returns all parts, laid end to end along the dimension named above; an argument that names none is the same for every part. Nothing has to cross between parts.
Inputs may be any that keep to these rules, and one draw needn't show every extreme that they name: `feature_token`: in every block of 128 consecutive features, each token number appears exactly 4 times.
All inputs are finite; a program needn't handle non-finite values.
Results may differ from the reference program's by a relative error of at most 0.018.
Values may be sent and summed in bfloat16 or wider, within the bound.
A program may use at most 128 MiB of HBM per device.

```python
import jax
import jax.numpy as jnp
from jax import lax

FEATS = 4096
RANK = 512
FEAT_TOKENS = 32
DIM = 1536
HIDDEN_SIZE = 3072
ROW_DEV = 16
ROW_GROUPS = 4
HIDDEN_BLOCKS = 4
ROWS = 64
TOKEN_FEATS = 128
HEAD_SIZE = 48


def shuffle_block(block_key):
    labels = jnp.arange(4 * FEAT_TOKENS, dtype=jnp.int32) // 4
    return jax.random.permutation(block_key, labels)


def draw_feature_token(key, part):
    key = jax.random.fold_in(key, 7)
    block_keys = jax.random.split(key, FEATS // (4 * FEAT_TOKENS))
    blocks = jax.vmap(shuffle_block)(block_keys)
    return blocks.reshape(FEATS).astype(jnp.int32)


def steps_of(rng, dims, cuts, low, top_value):
    def one(axis_at, shards_of):
        heights = jax.random.uniform(jax.random.fold_in(jax.random.fold_in(rng, 6), axis_at), (shards_of,), jnp.float32, low / len(cuts), top_value / len(cuts))
        return jnp.repeat(jnp.exp(heights), dims[axis_at] // shards_of).reshape((-1,) + (1,) * (len(dims) - axis_at - 1))

    factor_of = one(*cuts[0])
    for cut in cuts[1:]:
        factor_of = factor_of * one(*cut)
    return factor_of


def centred(stream_key, shape, deviation, most, pieces=(), kind=jnp.bfloat16):
    drawn = jax.random.normal(stream_key, shape, jnp.float32) * deviation
    if len(pieces) > 0:
        drawn = steps_of(stream_key, shape, pieces, -0.22, 0.18) * drawn
    return jnp.clip(drawn, min=-most, max=most).astype(kind)


def setup_inputs(seed: int = 0, part: int = 0) -> dict:
    streams_of = jax.random.split(jax.random.key(seed), 16)
    part_keys = jax.random.split(jax.random.fold_in(streams_of[15], part), 16)
    features = centred(part_keys[0], (ROWS, FEATS), 1.0, 6.0, ((0, 4), (1, 4)))
    cross_down = centred(streams_of[1], (FEATS, RANK), FEATS ** -0.5, 0.09375, ((0, 4),))
    cross_up = centred(streams_of[2], (RANK, FEATS), RANK ** -0.5, 0.25, ((1, 4),))
    cross_bias = centred(streams_of[3], (FEATS,), 1.0, 4.0, ((0, 4),), jnp.float32)
    feature_token = draw_feature_token(jax.random.fold_in(streams_of[15], 71), part)
    proj_weight = centred(streams_of[5], (FEAT_TOKENS, TOKEN_FEATS, DIM), TOKEN_FEATS ** -0.5, 0.5, ((0, 4),))
    proj_bias = centred(streams_of[6], (FEAT_TOKENS, DIM), 0.5, 3.0, ((0, 4),), jnp.float32)
    mix_gain = jnp.clip(1.0 + 0.18 * jax.random.normal(streams_of[7], (FEAT_TOKENS, DIM), jnp.float32), 0.1, 1.9)
    expand_weight = centred(streams_of[8], (FEAT_TOKENS, DIM, HIDDEN_SIZE), DIM ** -0.5, 0.15625, ((0, 4), (2, 4)))
    expand_bias = centred(streams_of[9], (FEAT_TOKENS, HIDDEN_SIZE), 0.5, 3.0, ((0, 4), (1, 4)), jnp.float32)
    contract_weight = centred(streams_of[10], (FEAT_TOKENS, HIDDEN_SIZE, DIM), HIDDEN_SIZE ** -0.5, 0.109375, ((0, 4), (1, 4)))
    contract_bias = centred(streams_of[11], (FEAT_TOKENS, DIM), 0.5, 3.0, ((0, 4),), jnp.float32)
    block_gain = jnp.clip(1.0 + 0.18 * jax.random.normal(streams_of[12], (FEAT_TOKENS, DIM), jnp.float32), 0.1, 1.9)
    gate_weight = centred(streams_of[13], (DIM, DIM), DIM ** -0.5, 0.15625, ((1, 4),))
    gate_bias = centred(streams_of[14], (DIM,), 1.0, 4.0, (), jnp.float32)
    return {"features": features, "cross_down": cross_down, "cross_up": cross_up, "cross_bias": cross_bias, "feature_token": feature_token, "proj_weight": proj_weight, "proj_bias": proj_bias, "mix_gain": mix_gain, "expand_weight": expand_weight, "expand_bias": expand_bias, "contract_weight": contract_weight, "contract_bias": contract_bias, "block_gain": block_gain, "gate_weight": gate_weight, "gate_bias": gate_bias}


def rms_norm(values, gain_row):
    scale = lax.rsqrt(lax.optimization_barrier(jnp.mean(values * values, axis=-1, keepdims=True)) + 1e-06)
    return values * scale * gain_row

def reference(features, cross_down, cross_up, cross_bias, feature_token, proj_weight, proj_bias, mix_gain, expand_weight, expand_bias, contract_weight, contract_bias, block_gain, gate_weight, gate_bias):
    low_rank = jnp.dot(features, cross_down, preferred_element_type=jnp.float32).astype(jnp.bfloat16)
    lifted = jnp.dot(low_rank, cross_up, preferred_element_type=jnp.float32)
    widened = features.astype(jnp.float32)
    crossed = (widened * (lifted + cross_bias) + widened).astype(jnp.bfloat16)
    ordering = jnp.argsort(feature_token, stable=True).astype(jnp.int32)
    picked = jnp.take(crossed, ordering, axis=1).reshape(ROWS, FEAT_TOKENS, TOKEN_FEATS)
    embedded = jnp.einsum('rtf,tfd->rtd', picked.astype(jnp.float32), proj_weight.astype(jnp.float32)) + proj_bias
    embedded = embedded.astype(jnp.bfloat16)
    mixed_heads = embedded.reshape(ROWS, FEAT_TOKENS, FEAT_TOKENS, HEAD_SIZE).transpose(0, 2, 1, 3).reshape(ROWS, FEAT_TOKENS, DIM)
    first_norm = rms_norm(mixed_heads.astype(jnp.float32) + embedded.astype(jnp.float32), mix_gain).astype(jnp.bfloat16)

    def token_network(operands):
        token_rows, weight_in, bias_in, weight_out = operands
        gelu_in = jnp.dot(token_rows, weight_in, preferred_element_type=jnp.float32) + bias_in
        activated = jax.nn.gelu(gelu_in).astype(jnp.bfloat16)
        partial_sums = jnp.einsum('rsh,shd->srd', activated.reshape(ROWS, HIDDEN_BLOCKS, -1).astype(jnp.float32), weight_out.reshape(HIDDEN_BLOCKS, -1, DIM).astype(jnp.float32))
        rounded = lax.optimization_barrier(partial_sums.astype(jnp.bfloat16))
        return lax.optimization_barrier(jnp.sum(rounded.astype(jnp.float32), axis=0))
    summed = lax.map(token_network, (first_norm.transpose(1, 0, 2), expand_weight, expand_bias, contract_weight))
    summed = summed.transpose(1, 0, 2) + contract_bias
    second_norm = rms_norm(summed + first_norm.astype(jnp.float32), block_gain).astype(jnp.bfloat16)
    logits = jnp.dot(second_norm.reshape(-1, DIM), gate_weight, preferred_element_type=jnp.float32).reshape(ROWS, FEAT_TOKENS, DIM)
    gated = (second_norm.astype(jnp.float32) * jax.nn.sigmoid(logits + gate_bias)).astype(jnp.bfloat16)
    return gated.reshape(ROW_GROUPS, ROW_DEV, FEAT_TOKENS, DIM)
```

```python
import functools

import jax
import jax.numpy as jnp
from jax import lax
from jax.experimental import pallas as pl
from jax.experimental.pallas import tpu as pltpu
from jax.sharding import PartitionSpec as P

FEAT_TOKENS = 32
DIM = 1536


def rms_norm(values, gain_row):
    scale = lax.rsqrt(jnp.mean(values * values, axis=-1, keepdims=True) + 1e-06)
    return values * scale * gain_row


def plain_device(
    features,
    cross_down,
    cross_up,
    cross_bias,
    feature_token,
    proj_weight,
    proj_bias,
    mix_gain,
    expand_weight,
    expand_bias,
    contract_weight,
    contract_bias,
    block_gain,
    gate_weight,
    gate_bias,
):
    rows_local = features.shape[0]
    local_tokens = proj_weight.shape[0]
    head_size = DIM // FEAT_TOKENS
    sources = lax.axis_size("tok")
    partial_low = jnp.dot(features, cross_down, preferred_element_type=jnp.float32)
    low_rank = lax.psum(partial_low.astype(jnp.bfloat16), "tok")
    lifted = jnp.dot(low_rank, cross_up, preferred_element_type=jnp.float32)
    widened = features.astype(jnp.float32)
    crossed = (widened * (lifted + cross_bias) + widened).astype(jnp.bfloat16)
    ordering = jnp.argsort(feature_token, stable=True)
    grouped = jnp.take(crossed, ordering, axis=1)
    routed = lax.all_to_all(grouped, "tok", split_axis=1, concat_axis=1, tiled=True)
    picked = (
        routed.reshape(rows_local, sources, local_tokens, -1)
        .transpose(0, 2, 1, 3)
        .reshape(rows_local, local_tokens, -1)
    )
    embedded = (
        jnp.einsum("rjf,jfd->rjd", picked, proj_weight, preferred_element_type=jnp.float32)
        + proj_bias
    )
    embedded = embedded.astype(jnp.bfloat16)
    heads_in = lax.all_to_all(embedded, "tok", split_axis=2, concat_axis=1, tiled=True)
    mixed_heads = (
        heads_in.reshape(rows_local, FEAT_TOKENS, local_tokens, head_size)
        .transpose(0, 2, 1, 3)
        .reshape(rows_local, local_tokens, DIM)
    )
    first_norm = rms_norm(
        mixed_heads.astype(jnp.float32) + embedded.astype(jnp.float32), mix_gain
    ).astype(jnp.bfloat16)
    every_row = lax.all_gather(first_norm, ("dp", "head"), axis=0, tiled=True)
    gelu_in = (
        jnp.einsum("rjd,jdh->rjh", every_row, expand_weight, preferred_element_type=jnp.float32)
        + expand_bias
    )
    activated = jax.nn.gelu(gelu_in).astype(jnp.bfloat16)
    summed = lax.psum_scatter(
        jnp.einsum(
            "rjh,jhd->rjd", activated, contract_weight, preferred_element_type=jnp.float32
        ).astype(jnp.bfloat16),
        ("dp", "head"),
        scatter_dimension=0,
        tiled=True,
    ).astype(jnp.float32)
    second_norm = rms_norm(
        summed + contract_bias + first_norm.astype(jnp.float32), block_gain
    ).astype(jnp.bfloat16)
    owned_rows = lax.all_to_all(second_norm, "tok", split_axis=0, concat_axis=1, tiled=True)
    flattened = owned_rows.reshape(-1, DIM)
    weight_piece = lax.all_gather(gate_weight, ("dp", "head"), axis=1, tiled=True)
    col_count = weight_piece.shape[1]
    logits = jnp.dot(flattened, weight_piece, preferred_element_type=jnp.float32).reshape(
        owned_rows.shape[0], owned_rows.shape[1], col_count
    )
    kept_cols = owned_rows.astype(jnp.float32)
    result = (kept_cols * jax.nn.sigmoid(logits + gate_bias)).astype(jnp.bfloat16)
    return result[None]


MESH = pl.DeviceIdType.MESH
F32 = jnp.float32
BF16 = jnp.bfloat16


def remote(src, dst, send_sem, recv_sem, device):
    return pltpu.make_async_remote_copy(
        src_ref=src, dst_ref=dst, send_sem=send_sem, recv_sem=recv_sem,
        device_id=device, device_id_type=MESH,
    )


def arrived(slot, send_sem, recv_sem, device):
    remote(slot, slot, send_sem, recv_sem, device).wait_recv()


def fused_kernel(
    toks, dps, heads,
    feat, cdown, cup, cbias, ftok, pbias, mgain, ebias, cbias2, bgain, gbias,
    gate_hbm, proj_hbm, exp_hbm, con_hbm,
    out,
    proj_v, exp_v, con_v, gate_v,
    low_buf, route_send, route_buf, picked, emb, head_buf, mixed, rows_v,
    part, sib_buf, xs_send, xs_buf, norm_rows, norm_send, norm_buf, perm,
    w_sem, gate_sem, gate_send, gate_recv, low_send, low_recv, rt_send, rt_recv,
    hd_send, hd_recv, ag_send, ag_recv, fw_send, sib_send, sib_recv, x_send, x_recv,
    nm_send, nm_recv,
):
    t = lax.axis_index("tok")
    p = lax.axis_index("dp")
    h = lax.axis_index("head")
    mine = p * heads + h
    here = h * dps + p
    local_tokens, _, dim = proj_v.shape
    rows_local = feat.shape[0]
    feats_local = feat.shape[1]
    wide = dim // toks
    total_tokens = toks * local_tokens
    head_size = dim // total_tokens
    sibling = {"head": 1 - h}

    def tok_at(q):
        return lax.rem(t + q, toks)

    def dp_at(q):
        return lax.rem(p + q, dps)

    def proj_copy(j):
        return pltpu.make_async_copy(proj_hbm.at[j], proj_v.at[j], w_sem.at[0, j])

    def exp_copy(j):
        return pltpu.make_async_copy(exp_hbm.at[j], exp_v.at[j], w_sem.at[1, j])

    def con_copy(j):
        return pltpu.make_async_copy(con_hbm.at[j], con_v.at[j], w_sem.at[2, j])

    gate_own = pltpu.make_async_copy(gate_hbm, gate_v.at[mine], gate_sem)
    gate_own.start()
    for j in range(local_tokens):
        proj_copy(j).start()
    for j in range(local_tokens):
        exp_copy(j).start()
        con_copy(j).start()

    barrier = pltpu.get_barrier_semaphore()
    for q in range(1, toks):
        pl.semaphore_signal(barrier, inc=1, device_id={"tok": tok_at(q)}, device_id_type=MESH)
    for q in range(1, dps):
        pl.semaphore_signal(barrier, inc=1, device_id={"dp": dp_at(q)}, device_id_type=MESH)
    pl.semaphore_signal(barrier, inc=1, device_id=sibling, device_id_type=MESH)

    low_buf[t] = jnp.dot(feat[...], cdown[...], preferred_element_type=F32)
    pl.semaphore_wait(barrier, toks - 1 + dps - 1 + 1)

    def low_copy(q):
        return remote(low_buf.at[t], low_buf.at[t], low_send.at[q], low_recv.at[t], {"tok": tok_at(q)})

    for q in range(1, toks):
        low_copy(q).start()

    gate_own.wait()

    def gate_copy(q):
        slot = gate_v.at[mine]
        device = sibling if q == 0 else {"dp": dp_at(q)}
        return remote(slot, slot, gate_send.at[q], gate_recv.at[mine], device)

    def gate_forward(q):
        source = dp_at(q) * heads + h
        slot = gate_v.at[source]
        return remote(slot, slot, gate_send.at[dps + q], gate_recv.at[source], sibling)

    for q in range(dps):
        gate_copy(q).start()

    lanes = 128
    share = feats_local // total_tokens
    feature_at = lax.broadcasted_iota(jnp.int32, (lanes, lanes), 0)
    feature_of = lax.broadcasted_iota(jnp.int32, (lanes, lanes), 1)
    place_at = lax.broadcasted_iota(jnp.int32, (feats_local, lanes), 0)
    per_block = lanes // total_tokens
    for b in range(feats_local // lanes):
        token_row = ftok[b : b + 1, :]
        across = jnp.broadcast_to(token_row, (lanes, lanes))
        along = across.astype(F32).T.astype(jnp.int32)
        earlier = jnp.logical_and(across == along, feature_at < feature_of)
        rank = jnp.sum(jnp.where(earlier, 1.0, 0.0), axis=0, keepdims=True).astype(jnp.int32)
        place = token_row * share + b * per_block + rank
        perm[:, b * lanes : (b + 1) * lanes] = jnp.where(place_at == place, 1.0, 0.0).astype(BF16)

    for q in range(1, toks):
        source = tok_at(q)
        arrived(low_buf.at[source], low_send.at[q], low_recv.at[source], {"tok": source})
    low = low_buf[0]
    for s in range(1, toks):
        low = low + low_buf[s]
    lifted = jnp.dot(low.astype(BF16), cup[...], preferred_element_type=F32)
    widened = feat[...].astype(F32)
    crossed = (widened * (lifted + cbias[...]) + widened).astype(BF16)
    grouped = lax.dot_general(
        crossed, perm[...], (((1,), (1,)), ((), ())), preferred_element_type=F32
    ).astype(BF16)
    span = feats_local // toks
    for s in range(toks):
        route_send[s] = grouped[:, s * span : (s + 1) * span]

    def route_copy(q):
        target = tok_at(q)
        return remote(route_send.at[target], route_buf.at[t], rt_send.at[q], rt_recv.at[t], {"tok": target})

    for q in range(1, toks):
        route_copy(q).start()
    route_buf[t] = route_send[t]
    for q in range(1, toks):
        source = tok_at(q)
        arrived(route_buf.at[source], rt_send.at[q], rt_recv.at[source], {"tok": source})
    for s in range(toks):
        for j in range(local_tokens):
            picked[j, :, s * share : (s + 1) * share] = route_buf[s, :, j * share : (j + 1) * share]

    def embed(j, carry):
        proj_copy(j).wait()
        value = jnp.dot(picked[j], proj_v[j], preferred_element_type=F32) + pbias[pl.ds(j, 1), :]
        value = value.astype(BF16)
        for s in range(toks):
            emb[s, j] = value[:, s * wide : (s + 1) * wide]
        return carry

    lax.fori_loop(0, local_tokens, embed, 0)

    def head_copy(q):
        target = tok_at(q)
        return remote(emb.at[target], head_buf.at[t], hd_send.at[q], hd_recv.at[t], {"tok": target})

    for q in range(1, toks):
        head_copy(q).start()
    head_buf[t] = emb[t]

    def turn(q, carry):
        source = tok_at(q)

        @pl.when(q > 0)
        def _():
            arrived(head_buf.at[source], hd_send.at[q], hd_recv.at[source], {"tok": source})

        for i in range(local_tokens):
            for k in range(local_tokens):
                mixed[source, k, :, i * head_size : (i + 1) * head_size] = head_buf[
                    source, i, :, k * head_size : (k + 1) * head_size
                ]
        return carry

    lax.fori_loop(0, toks, turn, 0)

    def gather_copy(j, q):
        slot = rows_v.at[j, here]
        device = sibling if q == 0 else {"dp": dp_at(q)}
        return remote(slot, slot, ag_send.at[j, q], ag_recv.at[j, here], device)

    def gather_forward(j, q):
        source = h * dps + dp_at(q)
        slot = rows_v.at[j, source]
        return remote(slot, slot, fw_send.at[j, q], ag_recv.at[j, source], sibling)

    def first(j, carry):
        sums = []
        square = jnp.zeros((rows_local, 1), F32)
        for s in range(toks):
            value = mixed[s, j].astype(F32) + emb[s, j].astype(F32)
            sums.append(value)
            square = square + jnp.sum(value * value, axis=1, keepdims=True)
        scale = lax.rsqrt(square * (1.0 / dim) + 1e-06)
        for s in range(toks):
            gain = mgain[pl.ds(j, 1), s * wide : (s + 1) * wide]
            rows_v[j, here, :, s * wide : (s + 1) * wide] = (sums[s] * scale * gain).astype(BF16)
        for q in range(dps):
            gather_copy(j, q).start()
        return carry

    lax.fori_loop(0, local_tokens, first, 0)

    def forward(j):
        for q in range(1, dps):
            source = h * dps + dp_at(q)
            arrived(rows_v.at[j, source], fw_send.at[j, q], ag_recv.at[j, source], sibling)
            gather_forward(j, q).start()

    def pair_copy(j):
        return remote(part.at[j, 1 - h], sib_buf.at[j], sib_send.at[j], sib_recv.at[j], sibling)

    def network(j):
        for q in range(dps):
            source = (1 - h) * dps + dp_at(q)
            arrived(rows_v.at[j, source], fw_send.at[j, q], ag_recv.at[j, source], sibling)
        exp_copy(j).wait()
        con_copy(j).wait()
        everything = rows_v[j].reshape(heads * dps * rows_local, dim)
        inner = jnp.dot(everything, exp_v[j], preferred_element_type=F32) + ebias[pl.ds(j, 1), :]
        active = jax.nn.gelu(inner).astype(BF16)
        sums = jnp.dot(active, con_v[j], preferred_element_type=F32).astype(BF16)
        part[j] = sums.reshape(heads, dps, rows_local, dim)
        pair_copy(j).start()

    def cross_copy(j, q):
        return remote(
            xs_send.at[j, q - 1], xs_buf.at[j, q - 1], x_send.at[j, q], x_recv.at[j, q], {"dp": dp_at(q)}
        )

    def combine(j):
        arrived(sib_buf.at[j], sib_send.at[j], sib_recv.at[j], sibling)
        for q in range(1, dps):
            target = dp_at(q)
            both = part[j, h, target].astype(F32) + sib_buf[j, target].astype(F32)
            xs_send[j, q - 1] = both.astype(BF16)
            cross_copy(j, q).start()

    def finish(j):
        total = part[j, h, p].astype(F32) + sib_buf[j, p].astype(F32)
        for q in range(1, dps):
            arrived(xs_buf.at[j, q - 1], x_send.at[j, q], x_recv.at[j, q], sibling)
            total = total + xs_buf[j, q - 1].astype(F32)
        total = total + cbias2[pl.ds(j, 1), :] + rows_v[j, here].astype(F32)
        scale = lax.rsqrt(jnp.sum(total * total, axis=1, keepdims=True) * (1.0 / dim) + 1e-06)
        value = total * scale * bgain[pl.ds(j, 1), :]
        for r in range(rows_local):
            norm_rows[r, pl.ds(j, 1), :] = value[r : r + 1, :]

    def step(i, carry):
        @pl.when(i < local_tokens)
        def _():
            forward(i)

        @pl.when(jnp.logical_and(i >= 1, i < local_tokens + 1))
        def _():
            network(i - 1)

        @pl.when(jnp.logical_and(i >= 2, i < local_tokens + 2))
        def _():
            combine(i - 2)

        @pl.when(i >= 4)
        def _():
            finish(i - 4)

        return carry

    lax.fori_loop(0, local_tokens + 4, step, 0)

    for q in range(1, dps):
        source = dp_at(q) * heads + h
        arrived(gate_v.at[source], gate_send.at[q], gate_recv.at[source], sibling)
        gate_forward(q).start()

    split_rows = rows_local // toks
    block = split_rows * local_tokens
    for s in range(toks):
        norm_send[s] = (
            norm_rows[s * split_rows : (s + 1) * split_rows].reshape(block, dim).astype(BF16)
        )

    def norm_copy(q):
        target = tok_at(q)
        return remote(norm_send.at[target], norm_buf.at[t], nm_send.at[q], nm_recv.at[t], {"tok": target})

    for q in range(1, toks):
        norm_copy(q).start()
    norm_buf[t] = norm_send[t]
    for q in range(dps):
        source = dp_at(q) * heads + (1 - h)
        arrived(gate_v.at[source], gate_send.at[q], gate_recv.at[source], sibling)
    for q in range(1, toks):
        source = tok_at(q)
        arrived(norm_buf.at[source], nm_send.at[q], nm_recv.at[source], {"tok": source})

    states = norm_buf[...].reshape(toks * block, dim)
    columns = gate_v.shape[2]
    for c in range(dps * heads):
        cut = slice(c * columns, (c + 1) * columns)
        logits = jnp.dot(states, gate_v[c], preferred_element_type=F32) + gbias[:, cut]
        kept = norm_buf[:, :, cut].reshape(toks * block, columns).astype(F32)
        gated = (kept * jax.nn.sigmoid(logits)).reshape(toks, split_rows, local_tokens, columns)
        for r in range(split_rows):
            out[0, r, :, cut] = gated[:, r].reshape(total_tokens, columns).astype(BF16)

    for q in range(1, toks):
        low_copy(q).wait_send()
        route_copy(q).wait_send()
        head_copy(q).wait_send()
        norm_copy(q).wait_send()
    for q in range(dps):
        gate_copy(q).wait_send()
    for q in range(1, dps):
        gate_forward(q).wait_send()

    def drain(j, carry):
        for q in range(dps):
            gather_copy(j, q).wait_send()
        for q in range(1, dps):
            gather_forward(j, q).wait_send()
            cross_copy(j, q).wait_send()
        pair_copy(j).wait_send()
        return carry

    lax.fori_loop(0, local_tokens, drain, 0)


def fused_device(
    features, cross_down, cross_up, cross_bias, feature_token, proj_weight, proj_bias,
    mix_gain, expand_weight, expand_bias, contract_weight, contract_bias, block_gain,
    gate_weight, gate_bias,
):
    toks, dps, heads = lax.axis_size("tok"), lax.axis_size("dp"), lax.axis_size("head")
    rows, feats = features.shape
    local, token_feats, dim = proj_weight.shape
    hidden = expand_weight.shape[2]
    wide = dim // toks
    split_rows = rows // toks
    block = split_rows * local
    vmem = pl.BlockSpec(memory_space=pltpu.VMEM)
    anywhere = pl.BlockSpec(memory_space=pl.ANY)
    dma = pltpu.SemaphoreType.DMA
    slots = heads * dps
    scratch = [
        pltpu.VMEM((local, token_feats, dim), BF16),
        pltpu.VMEM((local, dim, hidden), BF16),
        pltpu.VMEM((local, hidden, dim), BF16),
        pltpu.VMEM((slots,) + gate_weight.shape, BF16),
        pltpu.VMEM((toks, rows, cross_down.shape[1]), F32),
        pltpu.VMEM((toks, rows, feats // toks), BF16),
        pltpu.VMEM((toks, rows, feats // toks), BF16),
        pltpu.VMEM((local, rows, token_feats), BF16),
        pltpu.VMEM((toks, local, rows, wide), BF16),
        pltpu.VMEM((toks, local, rows, wide), BF16),
        pltpu.VMEM((toks, local, rows, wide), BF16),
        pltpu.VMEM((local, slots, rows, dim), BF16),
        pltpu.VMEM((local, heads, dps, rows, dim), BF16),
        pltpu.VMEM((local, dps, rows, dim), BF16),
        pltpu.VMEM((local, dps - 1, rows, dim), BF16),
        pltpu.VMEM((local, dps - 1, rows, dim), BF16),
        pltpu.VMEM((rows, local, dim), F32),
        pltpu.VMEM((toks, block, dim), BF16),
        pltpu.VMEM((toks, block, dim), BF16),
        pltpu.VMEM((feats, feats), BF16),
        dma((3, local)), dma, dma((2 * dps,)), dma((slots,)),
        dma((toks,)), dma((toks,)), dma((toks,)), dma((toks,)),
        dma((toks,)), dma((toks,)),
        dma((local, dps)), dma((local, slots)), dma((local, dps)),
        dma((local,)), dma((local,)), dma((local, dps)), dma((local, dps)),
        dma((toks,)), dma((toks,)),
    ]
    return pl.pallas_call(
        functools.partial(fused_kernel, toks, dps, heads),
        out_shape=jax.ShapeDtypeStruct((1, split_rows, toks * local, dim), BF16),
        in_specs=[vmem] * 11 + [anywhere] * 4,
        out_specs=vmem,
        scratch_shapes=scratch,
        compiler_params=pltpu.CompilerParams(
            collective_id=0, has_side_effects=True, vmem_limit_bytes=63 * 2**20
        ),
    )(
        features, cross_down, cross_up, cross_bias.reshape(1, -1),
        feature_token.reshape(-1, 128), proj_bias, mix_gain, expand_bias, contract_bias,
        block_gain, gate_bias.reshape(1, -1), gate_weight, proj_weight, expand_weight,
        contract_weight,
    )


def per_device(*arrays):
    features, gate_weight = arrays[0], arrays[13]
    toks = lax.axis_size("tok")
    local = arrays[5].shape[0]
    fits = (
        lax.axis_size("head") == 2
        and lax.axis_size("dp") > 1
        and (DIM // toks) % 128 == 0
        and gate_weight.shape[1] % 128 == 0
        and features.shape[0] % 16 == 0
        and features.shape[0] % toks == 0
        and (features.shape[1] // toks) % 128 == 0
        and features.shape[0] // toks * local % 16 == 0
        and local % 8 == 0
    )
    return (fused_device if fits else plain_device)(*arrays)


def solution(mesh):
    placed = (
        P(("groups", "dp", "head"), "tok"),
        P("tok", None),
        P(None, "tok"),
        P("tok"),
        P("tok"),
        P("tok", None, None),
        P("tok", None),
        P("tok", None),
        P("tok", None, ("dp", "head")),
        P("tok", ("dp", "head")),
        P("tok", ("dp", "head"), None),
        P("tok", None),
        P("tok", None),
        P(None, ("dp", "head")),
        P(),
    )
    return jax.shard_map(
        per_device,
        mesh=mesh,
        in_specs=placed,
        out_specs=P(("groups", "dp", "head"), "tok", None, None),
        check_vma=False,
    )
```

```python
import functools

import jax
import jax.numpy as jnp
from jax import lax
from jax.experimental import pallas as pl
from jax.experimental.pallas import tpu as pltpu
from jax.sharding import PartitionSpec as P

FEAT_TOKENS = 32
DIM = 1536


def rms_norm(values, gain_row):
    scale = lax.rsqrt(jnp.mean(values * values, axis=-1, keepdims=True) + 1e-06)
    return values * scale * gain_row


def plain_device(
    features,
    cross_down,
    cross_up,
    cross_bias,
    feature_token,
    proj_weight,
    proj_bias,
    mix_gain,
    expand_weight,
    expand_bias,
    contract_weight,
    contract_bias,
    block_gain,
    gate_weight,
    gate_bias,
):
    rows_local = features.shape[0]
    local_tokens = proj_weight.shape[0]
    head_size = DIM // FEAT_TOKENS
    sources = lax.axis_size("tok")
    partial_low = jnp.dot(features, cross_down, preferred_element_type=jnp.float32)
    low_rank = lax.psum(partial_low.astype(jnp.bfloat16), "tok")
    lifted = jnp.dot(low_rank, cross_up, preferred_element_type=jnp.float32)
    widened = features.astype(jnp.float32)
    crossed = (widened * (lifted + cross_bias) + widened).astype(jnp.bfloat16)
    ordering = jnp.argsort(feature_token, stable=True)
    grouped = jnp.take(crossed, ordering, axis=1)
    routed = lax.all_to_all(grouped, "tok", split_axis=1, concat_axis=1, tiled=True)
    picked = (
        routed.reshape(rows_local, sources, local_tokens, -1)
        .transpose(0, 2, 1, 3)
        .reshape(rows_local, local_tokens, -1)
    )
    embedded = (
        jnp.einsum("rjf,jfd->rjd", picked, proj_weight, preferred_element_type=jnp.float32)
        + proj_bias
    )
    embedded = embedded.astype(jnp.bfloat16)
    heads_in = lax.all_to_all(embedded, "tok", split_axis=2, concat_axis=1, tiled=True)
    mixed_heads = (
        heads_in.reshape(rows_local, FEAT_TOKENS, local_tokens, head_size)
        .transpose(0, 2, 1, 3)
        .reshape(rows_local, local_tokens, DIM)
    )
    first_norm = rms_norm(
        mixed_heads.astype(jnp.float32) + embedded.astype(jnp.float32), mix_gain
    ).astype(jnp.bfloat16)
    every_row = lax.all_gather(first_norm, ("dp", "head"), axis=0, tiled=True)
    gelu_in = (
        jnp.einsum("rjd,jdh->rjh", every_row, expand_weight, preferred_element_type=jnp.float32)
        + expand_bias
    )
    activated = jax.nn.gelu(gelu_in).astype(jnp.bfloat16)
    summed = lax.psum_scatter(
        jnp.einsum(
            "rjh,jhd->rjd", activated, contract_weight, preferred_element_type=jnp.float32
        ).astype(jnp.bfloat16),
        ("dp", "head"),
        scatter_dimension=0,
        tiled=True,
    ).astype(jnp.float32)
    second_norm = rms_norm(
        summed + contract_bias + first_norm.astype(jnp.float32), block_gain
    ).astype(jnp.bfloat16)
    owned_rows = lax.all_to_all(second_norm, "tok", split_axis=0, concat_axis=1, tiled=True)
    flattened = owned_rows.reshape(-1, DIM)
    weight_piece = lax.all_gather(gate_weight, ("dp", "head"), axis=1, tiled=True)
    col_count = weight_piece.shape[1]
    logits = jnp.dot(flattened, weight_piece, preferred_element_type=jnp.float32).reshape(
        owned_rows.shape[0], owned_rows.shape[1], col_count
    )
    kept_cols = owned_rows.astype(jnp.float32)
    result = (kept_cols * jax.nn.sigmoid(logits + gate_bias)).astype(jnp.bfloat16)
    return result[None]


MESH = pl.DeviceIdType.MESH
F32 = jnp.float32
BF16 = jnp.bfloat16


def remote(src, dst, send_sem, recv_sem, device):
    return pltpu.make_async_remote_copy(
        src_ref=src, dst_ref=dst, send_sem=send_sem, recv_sem=recv_sem,
        device_id=device, device_id_type=MESH,
    )


def arrived(slot, send_sem, recv_sem, device):
    remote(slot, slot, send_sem, recv_sem, device).wait_recv()


def fused_kernel(
    toks, dps, heads,
    feat, cdown, cup, cbias, ftok, pbias, mgain, ebias, cbias2, bgain, gbias,
    gate_hbm, proj_hbm, exp_hbm, con_hbm,
    out,
    proj_v, exp_v, con_v, gate_v,
    low_buf, route_send, route_buf, picked, emb, head_buf, mixed, rows_v,
    part, sib_buf, xs_send, xs_buf, norm_rows, norm_send, norm_buf, perm,
    w_sem, gate_sem, gate_send, gate_recv, low_send, low_recv, rt_send, rt_recv,
    hd_send, hd_recv, ag_send, ag_recv, fw_send, sib_send, sib_recv, x_send, x_recv,
    nm_send, nm_recv,
):
    t = lax.axis_index("tok")
    p = lax.axis_index("dp")
    h = lax.axis_index("head")
    u = lax.axis_index("groups")
    mine = p * heads + h
    here = h * dps + p
    local_tokens, _, dim = proj_v.shape
    rows_local = feat.shape[0]
    feats_local = feat.shape[1]
    wide = dim // toks
    total_tokens = toks * local_tokens
    head_size = dim // total_tokens
    sibling = {"head": 1 - h}
    replica = {"groups": 1 - u}

    def tok_at(q):
        return lax.rem(t + q, toks)

    def dp_at(q):
        return lax.rem(p + q, dps)

    def proj_copy(j):
        return pltpu.make_async_copy(proj_hbm.at[j], proj_v.at[j], w_sem.at[0, j])

    def exp_copy(j):
        return pltpu.make_async_copy(exp_hbm.at[j], exp_v.at[j], w_sem.at[1, j])

    def con_copy(j):
        return pltpu.make_async_copy(con_hbm.at[j], con_v.at[j], w_sem.at[2, j])

    gate_own = pltpu.make_async_copy(gate_hbm, gate_v.at[mine], gate_sem)
    gate_own.start()
    for j in range(local_tokens):
        proj_copy(j).start()

    barrier = pltpu.get_barrier_semaphore()
    for q in range(1, toks):
        pl.semaphore_signal(barrier, inc=1, device_id={"tok": tok_at(q)}, device_id_type=MESH)
    for q in range(1, dps):
        pl.semaphore_signal(barrier, inc=1, device_id={"dp": dp_at(q)}, device_id_type=MESH)
    pl.semaphore_signal(barrier, inc=1, device_id=sibling, device_id_type=MESH)
    pl.semaphore_signal(barrier, inc=1, device_id=replica, device_id_type=MESH)

    low_buf[t] = jnp.dot(feat[...], cdown[...], preferred_element_type=F32)
    pl.semaphore_wait(barrier, toks - 1 + dps - 1 + 2)

    def low_copy(q):
        return remote(low_buf.at[t], low_buf.at[t], low_send.at[q], low_recv.at[t], {"tok": tok_at(q)})

    for q in range(1, toks):
        low_copy(q).start()

    gate_own.wait()

    def gate_copy(q):
        if q == 0:
            slot = gate_v.at[mine]
            return remote(slot, slot, gate_send.at[0, q], gate_recv.at[mine, 0], sibling)
        slot = gate_v.at[mine, u]
        return remote(slot, slot, gate_send.at[0, q], gate_recv.at[mine, u], {"dp": dp_at(q)})

    def gate_forward(q, kind):
        source = dp_at(q) * heads + h
        half = 1 - u if kind == 3 else u
        device = replica if kind == 1 else sibling
        slot = gate_v.at[source, half]
        return remote(slot, slot, gate_send.at[kind, q], gate_recv.at[source, half], device)

    def gate_arrived(source, half):
        arrived(gate_v.at[source, half], gate_send.at[0, 0], gate_recv.at[source, half], sibling)

    for q in range(dps):
        gate_copy(q).start()

    lanes = 128
    share = feats_local // total_tokens
    feature_at = lax.broadcasted_iota(jnp.int32, (lanes, lanes), 0)
    feature_of = lax.broadcasted_iota(jnp.int32, (lanes, lanes), 1)
    place_at = lax.broadcasted_iota(jnp.int32, (feats_local, lanes), 0)
    per_block = lanes // total_tokens
    for b in range(feats_local // lanes):
        token_row = ftok[b : b + 1, :]
        across = jnp.broadcast_to(token_row, (lanes, lanes))
        along = across.astype(F32).T.astype(jnp.int32)
        earlier = jnp.logical_and(across == along, feature_at < feature_of)
        rank = jnp.sum(jnp.where(earlier, 1.0, 0.0), axis=0, keepdims=True).astype(jnp.int32)
        place = token_row * share + b * per_block + rank
        perm[:, b * lanes : (b + 1) * lanes] = jnp.where(place_at == place, 1.0, 0.0).astype(BF16)

    for q in range(1, toks):
        source = tok_at(q)
        arrived(low_buf.at[source], low_send.at[q], low_recv.at[source], {"tok": source})
    low = low_buf[0]
    for s in range(1, toks):
        low = low + low_buf[s]
    lifted = jnp.dot(low.astype(BF16), cup[...], preferred_element_type=F32)
    widened = feat[...].astype(F32)
    crossed = (widened * (lifted + cbias[...]) + widened).astype(BF16)
    grouped = lax.dot_general(
        crossed, perm[...], (((1,), (1,)), ((), ())), preferred_element_type=F32
    ).astype(BF16)
    span = feats_local // toks
    for s in range(toks):
        route_send[s] = grouped[:, s * span : (s + 1) * span]

    def route_copy(q):
        target = tok_at(q)
        return remote(route_send.at[target], route_buf.at[t], rt_send.at[q], rt_recv.at[t], {"tok": target})

    for q in range(1, toks):
        route_copy(q).start()
    route_buf[t] = route_send[t]
    for j in range(local_tokens):
        exp_copy(j).start()
        con_copy(j).start()
    for q in range(1, toks):
        source = tok_at(q)
        arrived(route_buf.at[source], rt_send.at[q], rt_recv.at[source], {"tok": source})
    for s in range(toks):
        for j in range(local_tokens):
            picked[j, :, s * share : (s + 1) * share] = route_buf[s, :, j * share : (j + 1) * share]

    def embed(j, carry):
        proj_copy(j).wait()
        value = jnp.dot(picked[j], proj_v[j], preferred_element_type=F32) + pbias[pl.ds(j, 1), :]
        value = value.astype(BF16)
        for s in range(toks):
            emb[s, j] = value[:, s * wide : (s + 1) * wide]
        return carry

    lax.fori_loop(0, local_tokens, embed, 0)

    def head_copy(q):
        target = tok_at(q)
        return remote(emb.at[target], head_buf.at[t], hd_send.at[q], hd_recv.at[t], {"tok": target})

    for q in range(1, toks):
        head_copy(q).start()
    head_buf[t] = emb[t]

    def turn(q, carry):
        source = tok_at(q)

        @pl.when(q > 0)
        def _():
            arrived(head_buf.at[source], hd_send.at[q], hd_recv.at[source], {"tok": source})

        for i in range(local_tokens):
            for k in range(local_tokens):
                mixed[source, k, :, i * head_size : (i + 1) * head_size] = head_buf[
                    source, i, :, k * head_size : (k + 1) * head_size
                ]
        return carry

    lax.fori_loop(0, toks, turn, 0)
    for q in range(1, dps):
        gate_arrived(dp_at(q) * heads + h, u)
        gate_forward(q, 1).start()
        gate_forward(q, 2).start()

    def gather_copy(j, q):
        slot = rows_v.at[j, here]
        device = sibling if q == 0 else {"dp": dp_at(q)}
        return remote(slot, slot, ag_send.at[j, q], ag_recv.at[j, here], device)

    def gather_forward(j, q):
        source = h * dps + dp_at(q)
        slot = rows_v.at[j, source]
        return remote(slot, slot, fw_send.at[j, q], ag_recv.at[j, source], sibling)

    def first(j, carry):
        sums = []
        square = jnp.zeros((rows_local, 1), F32)
        for s in range(toks):
            value = mixed[s, j].astype(F32) + emb[s, j].astype(F32)
            sums.append(value)
            square = square + jnp.sum(value * value, axis=1, keepdims=True)
        scale = lax.rsqrt(square * (1.0 / dim) + 1e-06)
        for s in range(toks):
            gain = mgain[pl.ds(j, 1), s * wide : (s + 1) * wide]
            rows_v[j, here, :, s * wide : (s + 1) * wide] = (sums[s] * scale * gain).astype(BF16)
        for q in range(dps):
            gather_copy(j, q).start()
        return carry

    lax.fori_loop(0, local_tokens, first, 0)

    def forward(j):
        for q in range(1, dps):
            source = h * dps + dp_at(q)
            arrived(rows_v.at[j, source], fw_send.at[j, q], ag_recv.at[j, source], sibling)
            gather_forward(j, q).start()

    def pair_copy(j):
        return remote(part.at[j, 1 - h], sib_buf.at[j], sib_send.at[j], sib_recv.at[j], sibling)

    def network(j):
        for q in range(dps):
            source = (1 - h) * dps + dp_at(q)
            arrived(rows_v.at[j, source], fw_send.at[j, q], ag_recv.at[j, source], sibling)
        exp_copy(j).wait()
        con_copy(j).wait()
        everything = rows_v[j].reshape(heads * dps * rows_local, dim)
        inner = jnp.dot(everything, exp_v[j], preferred_element_type=F32) + ebias[pl.ds(j, 1), :]
        active = jax.nn.gelu(inner).astype(BF16)
        sums = jnp.dot(active, con_v[j], preferred_element_type=F32).astype(BF16)
        part[j] = sums.reshape(heads, dps, rows_local, dim)
        pair_copy(j).start()

    def cross_copy(j, q):
        return remote(
            xs_send.at[j, q - 1], xs_buf.at[j, q - 1], x_send.at[j, q], x_recv.at[j, q], {"dp": dp_at(q)}
        )

    def combine(j):
        arrived(sib_buf.at[j], sib_send.at[j], sib_recv.at[j], sibling)
        for q in range(1, dps):
            target = dp_at(q)
            both = part[j, h, target].astype(F32) + sib_buf[j, target].astype(F32)
            xs_send[j, q - 1] = both.astype(BF16)
            cross_copy(j, q).start()

    def finish(j):
        total = part[j, h, p].astype(F32) + sib_buf[j, p].astype(F32)
        for q in range(1, dps):
            arrived(xs_buf.at[j, q - 1], x_send.at[j, q], x_recv.at[j, q], sibling)
            total = total + xs_buf[j, q - 1].astype(F32)
        total = total + cbias2[pl.ds(j, 1), :] + rows_v[j, here].astype(F32)
        scale = lax.rsqrt(jnp.sum(total * total, axis=1, keepdims=True) * (1.0 / dim) + 1e-06)
        value = total * scale * bgain[pl.ds(j, 1), :]
        for r in range(rows_local):
            norm_rows[r, pl.ds(j, 1), :] = value[r : r + 1, :]

    def step(i, carry):
        @pl.when(i < local_tokens)
        def _():
            forward(i)

        @pl.when(jnp.logical_and(i >= 1, i < local_tokens + 1))
        def _():
            network(i - 1)

        @pl.when(jnp.logical_and(i >= 2, i < local_tokens + 2))
        def _():
            combine(i - 2)

        @pl.when(i >= 4)
        def _():
            finish(i - 4)

        return carry

    lax.fori_loop(0, local_tokens + 4, step, 0)

    for q in range(1, dps):
        gate_arrived(dp_at(q) * heads + h, 1 - u)
        gate_forward(q, 3).start()

    split_rows = rows_local // toks
    block = split_rows * local_tokens
    for s in range(toks):
        norm_send[s] = (
            norm_rows[s * split_rows : (s + 1) * split_rows].reshape(block, dim).astype(BF16)
        )

    def norm_copy(q):
        target = tok_at(q)
        return remote(norm_send.at[target], norm_buf.at[t], nm_send.at[q], nm_recv.at[t], {"tok": target})

    for q in range(1, toks):
        norm_copy(q).start()
    norm_buf[t] = norm_send[t]
    beside = gate_v.at[p * heads + (1 - h)]
    arrived(beside, gate_send.at[0, 0], gate_recv.at[p * heads + (1 - h), 0], sibling)
    for q in range(1, dps):
        for half in range(2):
            gate_arrived(dp_at(q) * heads + (1 - h), half)
    for q in range(1, toks):
        source = tok_at(q)
        arrived(norm_buf.at[source], nm_send.at[q], nm_recv.at[source], {"tok": source})

    gate_row = gbias[...].reshape(1, dim)
    states = norm_buf[...].reshape(toks * block, dim)
    columns = gate_v.shape[3]
    for c in range(dps * heads):
        cut = slice(c * columns, (c + 1) * columns)
        logits = jnp.dot(states, gate_v[c].reshape(dim, columns), preferred_element_type=F32) + gate_row[:, cut]
        kept = norm_buf[:, :, cut].reshape(toks * block, columns).astype(F32)
        gated = (kept * jax.nn.sigmoid(logits)).reshape(toks, split_rows, local_tokens, columns)
        for r in range(split_rows):
            out[0, r, :, cut] = gated[:, r].reshape(total_tokens, columns).astype(BF16)

    for q in range(1, toks):
        low_copy(q).wait_send()
        route_copy(q).wait_send()
        head_copy(q).wait_send()
        norm_copy(q).wait_send()
    for q in range(dps):
        gate_copy(q).wait_send()
    for q in range(1, dps):
        for kind in range(1, 4):
            gate_forward(q, kind).wait_send()

    def drain(j, carry):
        for q in range(dps):
            gather_copy(j, q).wait_send()
        for q in range(1, dps):
            gather_forward(j, q).wait_send()
            cross_copy(j, q).wait_send()
        pair_copy(j).wait_send()
        return carry

    lax.fori_loop(0, local_tokens, drain, 0)


def fused_device(
    features, cross_down, cross_up, cross_bias, feature_token, proj_weight, proj_bias,
    mix_gain, expand_weight, expand_bias, contract_weight, contract_bias, block_gain,
    gate_weight, gate_bias,
):
    toks, dps, heads = lax.axis_size("tok"), lax.axis_size("dp"), lax.axis_size("head")
    rows, feats = features.shape
    local, token_feats, dim = proj_weight.shape
    hidden = expand_weight.shape[2]
    wide = dim // toks
    split_rows = rows // toks
    block = split_rows * local
    vmem = pl.BlockSpec(memory_space=pltpu.VMEM)
    anywhere = pl.BlockSpec(memory_space=pl.ANY)
    dma = pltpu.SemaphoreType.DMA
    slots = heads * dps
    scratch = [
        pltpu.VMEM((local, token_feats, dim), BF16),
        pltpu.VMEM((local, dim, hidden), BF16),
        pltpu.VMEM((local, hidden, dim), BF16),
        pltpu.VMEM((slots, 2, dim // 2, gate_weight.shape[1]), BF16),
        pltpu.VMEM((toks, rows, cross_down.shape[1]), F32),
        pltpu.VMEM((toks, rows, feats // toks), BF16),
        pltpu.VMEM((toks, rows, feats // toks), BF16),
        pltpu.VMEM((local, rows, token_feats), BF16),
        pltpu.VMEM((toks, local, rows, wide), BF16),
        pltpu.VMEM((toks, local, rows, wide), BF16),
        pltpu.VMEM((toks, local, rows, wide), BF16),
        pltpu.VMEM((local, slots, rows, dim), BF16),
        pltpu.VMEM((local, heads, dps, rows, dim), BF16),
        pltpu.VMEM((local, dps, rows, dim), BF16),
        pltpu.VMEM((local, dps - 1, rows, dim), BF16),
        pltpu.VMEM((local, dps - 1, rows, dim), BF16),
        pltpu.VMEM((rows, local, dim), F32),
        pltpu.VMEM((toks, block, dim), BF16),
        pltpu.VMEM((toks, block, dim), BF16),
        pltpu.VMEM((feats, feats), BF16),
        dma((3, local)), dma, dma((4, dps)), dma((slots, 2)),
        dma((toks,)), dma((toks,)), dma((toks,)), dma((toks,)),
        dma((toks,)), dma((toks,)),
        dma((local, dps)), dma((local, slots)), dma((local, dps)),
        dma((local,)), dma((local,)), dma((local, dps)), dma((local, dps)),
        dma((toks,)), dma((toks,)),
    ]
    gate_halves = gate_weight.reshape(2, -1, gate_weight.shape[1])
    return pl.pallas_call(
        functools.partial(fused_kernel, toks, dps, heads),
        out_shape=jax.ShapeDtypeStruct((1, split_rows, toks * local, dim), BF16),
        in_specs=[vmem] * 11 + [anywhere] * 4,
        out_specs=vmem,
        scratch_shapes=scratch,
        compiler_params=pltpu.CompilerParams(
            collective_id=0, has_side_effects=True, vmem_limit_bytes=63 * 2**20
        ),
    )(
        features, cross_down, cross_up, cross_bias.reshape(1, -1),
        feature_token.reshape(-1, 128), proj_bias, mix_gain, expand_bias, contract_bias,
        block_gain, gate_bias, gate_halves, proj_weight, expand_weight,
        contract_weight,
    )


def per_device(*arrays):
    features, gate_weight = arrays[0], arrays[13]
    toks = lax.axis_size("tok")
    local = arrays[5].shape[0]
    fits = (
        lax.axis_size("head") == 2
        and lax.axis_size("groups") == 2
        and lax.axis_size("dp") > 1
        and (DIM // toks) % 128 == 0
        and gate_weight.shape[1] % 128 == 0
        and features.shape[0] % 16 == 0
        and features.shape[0] % toks == 0
        and (features.shape[1] // toks) % 128 == 0
        and features.shape[0] // toks * local % 16 == 0
        and local % 8 == 0
    )
    return (fused_device if fits else plain_device)(*arrays)


def solution(mesh):
    placed = (
        P(("groups", "dp", "head"), "tok"),
        P("tok", None),
        P(None, "tok"),
        P("tok"),
        P("tok"),
        P("tok", None, None),
        P("tok", None),
        P("tok", None),
        P("tok", None, ("dp", "head")),
        P("tok", ("dp", "head")),
        P("tok", ("dp", "head"), None),
        P("tok", None),
        P("tok", None),
        P(None, ("dp", "head")),
        P(),
    )
    return jax.shard_map(
        per_device,
        mesh=mesh,
        in_specs=placed,
        out_specs=P(("groups", "dp", "head"), "tok", None, None),
        check_vma=False,
    )
```

```python
import functools

import jax
import jax.numpy as jnp
from jax import lax
from jax.experimental import pallas as pl
from jax.experimental.pallas import tpu as pltpu
from jax.sharding import PartitionSpec as P

FEAT_TOKENS = 32
DIM = 1536


def rms_norm(values, gain_row):
    scale = lax.rsqrt(jnp.mean(values * values, axis=-1, keepdims=True) + 1e-06)
    return values * scale * gain_row


def plain_device(
    features,
    cross_down,
    cross_up,
    cross_bias,
    feature_token,
    proj_weight,
    proj_bias,
    mix_gain,
    expand_weight,
    expand_bias,
    contract_weight,
    contract_bias,
    block_gain,
    gate_weight,
    gate_bias,
):
    rows_local = features.shape[0]
    local_tokens = proj_weight.shape[0]
    head_size = DIM // FEAT_TOKENS
    sources = lax.axis_size("tok")
    partial_low = jnp.dot(features, cross_down, preferred_element_type=jnp.float32)
    low_rank = lax.psum(partial_low.astype(jnp.bfloat16), "tok")
    lifted = jnp.dot(low_rank, cross_up, preferred_element_type=jnp.float32)
    widened = features.astype(jnp.float32)
    crossed = (widened * (lifted + cross_bias) + widened).astype(jnp.bfloat16)
    ordering = jnp.argsort(feature_token, stable=True)
    grouped = jnp.take(crossed, ordering, axis=1)
    routed = lax.all_to_all(grouped, "tok", split_axis=1, concat_axis=1, tiled=True)
    picked = (
        routed.reshape(rows_local, sources, local_tokens, -1)
        .transpose(0, 2, 1, 3)
        .reshape(rows_local, local_tokens, -1)
    )
    embedded = (
        jnp.einsum("rjf,jfd->rjd", picked, proj_weight, preferred_element_type=jnp.float32)
        + proj_bias
    )
    embedded = embedded.astype(jnp.bfloat16)
    heads_in = lax.all_to_all(embedded, "tok", split_axis=2, concat_axis=1, tiled=True)
    mixed_heads = (
        heads_in.reshape(rows_local, FEAT_TOKENS, local_tokens, head_size)
        .transpose(0, 2, 1, 3)
        .reshape(rows_local, local_tokens, DIM)
    )
    first_norm = rms_norm(
        mixed_heads.astype(jnp.float32) + embedded.astype(jnp.float32), mix_gain
    ).astype(jnp.bfloat16)
    every_row = lax.all_gather(first_norm, ("dp", "head"), axis=0, tiled=True)
    gelu_in = (
        jnp.einsum("rjd,jdh->rjh", every_row, expand_weight, preferred_element_type=jnp.float32)
        + expand_bias
    )
    activated = jax.nn.gelu(gelu_in).astype(jnp.bfloat16)
    summed = lax.psum_scatter(
        jnp.einsum(
            "rjh,jhd->rjd", activated, contract_weight, preferred_element_type=jnp.float32
        ).astype(jnp.bfloat16),
        ("dp", "head"),
        scatter_dimension=0,
        tiled=True,
    ).astype(jnp.float32)
    second_norm = rms_norm(
        summed + contract_bias + first_norm.astype(jnp.float32), block_gain
    ).astype(jnp.bfloat16)
    owned_rows = lax.all_to_all(second_norm, "tok", split_axis=0, concat_axis=1, tiled=True)
    flattened = owned_rows.reshape(-1, DIM)
    weight_piece = lax.all_gather(gate_weight, ("dp", "head"), axis=1, tiled=True)
    col_count = weight_piece.shape[1]
    logits = jnp.dot(flattened, weight_piece, preferred_element_type=jnp.float32).reshape(
        owned_rows.shape[0], owned_rows.shape[1], col_count
    )
    kept_cols = owned_rows.astype(jnp.float32)
    result = (kept_cols * jax.nn.sigmoid(logits + gate_bias)).astype(jnp.bfloat16)
    return result[None]


MESH = pl.DeviceIdType.MESH
F32 = jnp.float32
BF16 = jnp.bfloat16


def remote(src, dst, send_sem, recv_sem, device):
    return pltpu.make_async_remote_copy(
        src_ref=src, dst_ref=dst, send_sem=send_sem, recv_sem=recv_sem,
        device_id=device, device_id_type=MESH,
    )


def arrived(slot, send_sem, recv_sem, device):
    remote(slot, slot, send_sem, recv_sem, device).wait_recv()


def fused_kernel(
    toks, dps, heads,
    feat, cdown, cup, cbias, ftok, pbias, mgain, ebias, cbias2, bgain, gbias,
    gate_hbm, proj_hbm, exp_hbm, con_hbm,
    out,
    proj_v, exp_v, con_v, gate_v,
    low_buf, route_send, route_buf, picked, emb, head_buf, mixed, rows_v,
    part, sib_buf, xs_send, xs_buf, norm_rows, norm_send, norm_buf, perm,
    w_sem, gate_sem, gate_send, gate_recv, low_send, low_recv, rt_send, rt_recv,
    hd_send, hd_recv, ag_send, ag_recv, fw_send, sib_send, sib_recv, x_send, x_recv,
    nm_send, nm_recv,
):
    t = lax.axis_index("tok")
    p = lax.axis_index("dp")
    h = lax.axis_index("head")
    u = lax.axis_index("groups")
    mine = p * heads + h
    here = h * dps + p
    local_tokens, _, dim = proj_v.shape
    rows_local = feat.shape[0]
    feats_local = feat.shape[1]
    wide = dim // toks
    total_tokens = toks * local_tokens
    head_size = dim // total_tokens
    sibling = {"head": 1 - h}
    replica = {"groups": 1 - u}

    def tok_at(q):
        return lax.rem(t + q, toks)

    def dp_at(q):
        return lax.rem(p + q, dps)

    def proj_copy(j):
        return pltpu.make_async_copy(proj_hbm.at[j], proj_v.at[j], w_sem.at[0, j])

    def exp_copy(j):
        return pltpu.make_async_copy(exp_hbm.at[j], exp_v.at[j], w_sem.at[1, j])

    def con_copy(j):
        return pltpu.make_async_copy(con_hbm.at[j], con_v.at[j], w_sem.at[2, j])

    gate_own = pltpu.make_async_copy(gate_hbm, gate_v.at[mine], gate_sem)
    gate_own.start()
    for j in range(local_tokens):
        proj_copy(j).start()

    barrier = pltpu.get_barrier_semaphore()
    for q in range(1, toks):
        pl.semaphore_signal(barrier, inc=1, device_id={"tok": tok_at(q)}, device_id_type=MESH)
    for q in range(1, dps):
        pl.semaphore_signal(barrier, inc=1, device_id={"dp": dp_at(q)}, device_id_type=MESH)
    pl.semaphore_signal(barrier, inc=1, device_id=sibling, device_id_type=MESH)
    pl.semaphore_signal(barrier, inc=1, device_id=replica, device_id_type=MESH)

    low_buf[t] = jnp.dot(feat[...], cdown[...], preferred_element_type=F32)
    pl.semaphore_wait(barrier, toks - 1 + dps - 1 + 2)

    def low_copy(q):
        return remote(low_buf.at[t], low_buf.at[t], low_send.at[q], low_recv.at[t], {"tok": tok_at(q)})

    for q in range(1, toks):
        low_copy(q).start()

    gate_own.wait()

    def gate_copy(q):
        if q == 0:
            slot = gate_v.at[mine]
            return remote(slot, slot, gate_send.at[0, q], gate_recv.at[mine, 0], sibling)
        slot = gate_v.at[mine, u]
        return remote(slot, slot, gate_send.at[0, q], gate_recv.at[mine, u], {"dp": dp_at(q)})

    def gate_forward(q, kind):
        source = dp_at(q) * heads + h
        half = 1 - u if kind == 3 else u
        device = replica if kind == 1 else sibling
        slot = gate_v.at[source, half]
        return remote(slot, slot, gate_send.at[kind, q], gate_recv.at[source, half], device)

    def gate_arrived(source, half):
        arrived(gate_v.at[source, half], gate_send.at[0, 0], gate_recv.at[source, half], sibling)

    for q in range(dps):
        gate_copy(q).start()

    lanes = 128
    share = feats_local // total_tokens
    feature_at = lax.broadcasted_iota(jnp.int32, (lanes, lanes), 0)
    feature_of = lax.broadcasted_iota(jnp.int32, (lanes, lanes), 1)
    place_at = lax.broadcasted_iota(jnp.int32, (feats_local, lanes), 0)
    per_block = lanes // total_tokens
    for b in range(feats_local // lanes):
        token_row = ftok[b : b + 1, :]
        across = jnp.broadcast_to(token_row, (lanes, lanes))
        along = across.astype(F32).T.astype(jnp.int32)
        earlier = jnp.logical_and(across == along, feature_at < feature_of)
        rank = jnp.sum(jnp.where(earlier, 1.0, 0.0), axis=0, keepdims=True).astype(jnp.int32)
        place = token_row * share + b * per_block + rank
        perm[:, b * lanes : (b + 1) * lanes] = jnp.where(place_at == place, 1.0, 0.0).astype(BF16)

    for q in range(1, toks):
        source = tok_at(q)
        arrived(low_buf.at[source], low_send.at[q], low_recv.at[source], {"tok": source})
    low = low_buf[0]
    for s in range(1, toks):
        low = low + low_buf[s]
    lifted = jnp.dot(low.astype(BF16), cup[...], preferred_element_type=F32)
    widened = feat[...].astype(F32)
    crossed = (widened * (lifted + cbias[...]) + widened).astype(BF16)
    grouped = lax.dot_general(
        crossed, perm[...], (((1,), (1,)), ((), ())), preferred_element_type=F32
    ).astype(BF16)
    span = feats_local // toks
    for s in range(toks):
        route_send[s] = grouped[:, s * span : (s + 1) * span]

    def route_copy(q):
        target = tok_at(q)
        return remote(route_send.at[target], route_buf.at[t], rt_send.at[q], rt_recv.at[t], {"tok": target})

    for q in range(1, toks):
        route_copy(q).start()
    route_buf[t] = route_send[t]
    for j in range(local_tokens):
        exp_copy(j).start()
        con_copy(j).start()
    for q in range(1, toks):
        source = tok_at(q)
        arrived(route_buf.at[source], rt_send.at[q], rt_recv.at[source], {"tok": source})
    for s in range(toks):
        for j in range(local_tokens):
            picked[j, :, s * share : (s + 1) * share] = route_buf[s, :, j * share : (j + 1) * share]

    def embed(j, carry):
        proj_copy(j).wait()
        value = jnp.dot(picked[j], proj_v[j], preferred_element_type=F32) + pbias[pl.ds(j, 1), :]
        value = value.astype(BF16)
        for s in range(toks):
            emb[s, j] = value[:, s * wide : (s + 1) * wide]
        return carry

    lax.fori_loop(0, local_tokens, embed, 0)

    chunk = 2
    chunks = local_tokens // chunk

    def head_copy(q, c):
        target = tok_at(q)
        cut = pl.ds(c * chunk, chunk)
        return remote(
            head_buf.at[target, cut], mixed.at[t, cut], hd_send.at[q, c], hd_recv.at[t, c], {"tok": target}
        )

    for c in range(chunks):

        def turn(target, carry):
            for k in range(c * chunk, (c + 1) * chunk):
                for i in range(local_tokens):
                    head_buf[target, k, :, i * head_size : (i + 1) * head_size] = emb[
                        target, i, :, k * head_size : (k + 1) * head_size
                    ]
            return carry

        lax.fori_loop(0, toks, turn, 0)
        for q in range(1, toks):
            head_copy(q, c).start()
    mixed[t] = head_buf[t]

    for q in range(1, dps):
        gate_arrived(dp_at(q) * heads + h, u)
        gate_forward(q, 1).start()
        gate_forward(q, 2).start()

    def gather_copy(j, q):
        slot = rows_v.at[j, here]
        device = sibling if q == 0 else {"dp": dp_at(q)}
        return remote(slot, slot, ag_send.at[j, q], ag_recv.at[j, here], device)

    def gather_forward(j, q):
        source = h * dps + dp_at(q)
        slot = rows_v.at[j, source]
        return remote(slot, slot, fw_send.at[j, q], ag_recv.at[j, source], sibling)

    def first(j, carry):
        sums = []
        square = jnp.zeros((rows_local, 1), F32)
        for s in range(toks):
            value = mixed[s, j].astype(F32) + emb[s, j].astype(F32)
            sums.append(value)
            square = square + jnp.sum(value * value, axis=1, keepdims=True)
        scale = lax.rsqrt(square * (1.0 / dim) + 1e-06)
        for s in range(toks):
            gain = mgain[pl.ds(j, 1), s * wide : (s + 1) * wide]
            rows_v[j, here, :, s * wide : (s + 1) * wide] = (sums[s] * scale * gain).astype(BF16)
        for q in range(dps):
            gather_copy(j, q).start()
        return carry

    for c in range(chunks):
        for q in range(1, toks):
            source = tok_at(q)
            slot = mixed.at[source, pl.ds(c * chunk, chunk)]
            arrived(slot, hd_send.at[q, c], hd_recv.at[source, c], {"tok": source})
        lax.fori_loop(c * chunk, (c + 1) * chunk, first, 0)

    def forward(j):
        for q in range(1, dps):
            source = h * dps + dp_at(q)
            arrived(rows_v.at[j, source], fw_send.at[j, q], ag_recv.at[j, source], sibling)
            gather_forward(j, q).start()

    def pair_copy(j):
        return remote(part.at[j, 1 - h], sib_buf.at[j], sib_send.at[j], sib_recv.at[j], sibling)

    def network(j):
        for q in range(dps):
            source = (1 - h) * dps + dp_at(q)
            arrived(rows_v.at[j, source], fw_send.at[j, q], ag_recv.at[j, source], sibling)
        exp_copy(j).wait()
        con_copy(j).wait()
        everything = rows_v[j].reshape(heads * dps * rows_local, dim)
        inner = jnp.dot(everything, exp_v[j], preferred_element_type=F32) + ebias[pl.ds(j, 1), :]
        active = jax.nn.gelu(inner).astype(BF16)
        sums = jnp.dot(active, con_v[j], preferred_element_type=F32).astype(BF16)
        part[j] = sums.reshape(heads, dps, rows_local, dim)
        pair_copy(j).start()

    def cross_copy(j, q):
        return remote(
            xs_send.at[j, q - 1], xs_buf.at[j, q - 1], x_send.at[j, q], x_recv.at[j, q], {"dp": dp_at(q)}
        )

    def combine(j):
        arrived(sib_buf.at[j], sib_send.at[j], sib_recv.at[j], sibling)
        for q in range(1, dps):
            target = dp_at(q)
            both = part[j, h, target].astype(F32) + sib_buf[j, target].astype(F32)
            xs_send[j, q - 1] = both.astype(BF16)
            cross_copy(j, q).start()

    def finish(j):
        total = part[j, h, p].astype(F32) + sib_buf[j, p].astype(F32)
        for q in range(1, dps):
            arrived(xs_buf.at[j, q - 1], x_send.at[j, q], x_recv.at[j, q], sibling)
            total = total + xs_buf[j, q - 1].astype(F32)
        total = total + cbias2[pl.ds(j, 1), :] + rows_v[j, here].astype(F32)
        scale = lax.rsqrt(jnp.sum(total * total, axis=1, keepdims=True) * (1.0 / dim) + 1e-06)
        value = total * scale * bgain[pl.ds(j, 1), :]
        for r in range(rows_local):
            norm_rows[r, pl.ds(j, 1), :] = value[r : r + 1, :]

    def step(i, carry):
        @pl.when(i < local_tokens)
        def _():
            forward(i)

        @pl.when(jnp.logical_and(i >= 1, i < local_tokens + 1))
        def _():
            network(i - 1)

        @pl.when(jnp.logical_and(i >= 2, i < local_tokens + 2))
        def _():
            combine(i - 2)

        @pl.when(i >= 4)
        def _():
            finish(i - 4)

        return carry

    lax.fori_loop(0, local_tokens + 4, step, 0)

    for q in range(1, dps):
        gate_arrived(dp_at(q) * heads + h, 1 - u)
        gate_forward(q, 3).start()

    split_rows = rows_local // toks
    block = split_rows * local_tokens
    for s in range(toks):
        norm_send[s] = (
            norm_rows[s * split_rows : (s + 1) * split_rows].reshape(block, dim).astype(BF16)
        )

    def norm_copy(q):
        target = tok_at(q)
        return remote(norm_send.at[target], norm_buf.at[t], nm_send.at[q], nm_recv.at[t], {"tok": target})

    for q in range(1, toks):
        norm_copy(q).start()
    norm_buf[t] = norm_send[t]
    beside = gate_v.at[p * heads + (1 - h)]
    arrived(beside, gate_send.at[0, 0], gate_recv.at[p * heads + (1 - h), 0], sibling)
    for q in range(1, dps):
        for half in range(2):
            gate_arrived(dp_at(q) * heads + (1 - h), half)
    for q in range(1, toks):
        source = tok_at(q)
        arrived(norm_buf.at[source], nm_send.at[q], nm_recv.at[source], {"tok": source})

    gate_row = gbias[...].reshape(1, dim)
    states = norm_buf[...].reshape(toks * block, dim)
    columns = gate_v.shape[3]
    for c in range(dps * heads):
        cut = slice(c * columns, (c + 1) * columns)
        logits = jnp.dot(states, gate_v[c].reshape(dim, columns), preferred_element_type=F32) + gate_row[:, cut]
        kept = norm_buf[:, :, cut].reshape(toks * block, columns).astype(F32)
        gated = (kept * jax.nn.sigmoid(logits)).reshape(toks, split_rows, local_tokens, columns)
        for r in range(split_rows):
            out[0, r, :, cut] = gated[:, r].reshape(total_tokens, columns).astype(BF16)

    for q in range(1, toks):
        low_copy(q).wait_send()
        route_copy(q).wait_send()
        for c in range(chunks):
            head_copy(q, c).wait_send()
        norm_copy(q).wait_send()
    for q in range(dps):
        gate_copy(q).wait_send()
    for q in range(1, dps):
        for kind in range(1, 4):
            gate_forward(q, kind).wait_send()

    def drain(j, carry):
        for q in range(dps):
            gather_copy(j, q).wait_send()
        for q in range(1, dps):
            gather_forward(j, q).wait_send()
            cross_copy(j, q).wait_send()
        pair_copy(j).wait_send()
        return carry

    lax.fori_loop(0, local_tokens, drain, 0)


def fused_device(
    features, cross_down, cross_up, cross_bias, feature_token, proj_weight, proj_bias,
    mix_gain, expand_weight, expand_bias, contract_weight, contract_bias, block_gain,
    gate_weight, gate_bias,
):
    toks, dps, heads = lax.axis_size("tok"), lax.axis_size("dp"), lax.axis_size("head")
    rows, feats = features.shape
    local, token_feats, dim = proj_weight.shape
    hidden = expand_weight.shape[2]
    wide = dim // toks
    split_rows = rows // toks
    block = split_rows * local
    vmem = pl.BlockSpec(memory_space=pltpu.VMEM)
    anywhere = pl.BlockSpec(memory_space=pl.ANY)
    dma = pltpu.SemaphoreType.DMA
    slots = heads * dps
    scratch = [
        pltpu.VMEM((local, token_feats, dim), BF16),
        pltpu.VMEM((local, dim, hidden), BF16),
        pltpu.VMEM((local, hidden, dim), BF16),
        pltpu.VMEM((slots, 2, dim // 2, gate_weight.shape[1]), BF16),
        pltpu.VMEM((toks, rows, cross_down.shape[1]), F32),
        pltpu.VMEM((toks, rows, feats // toks), BF16),
        pltpu.VMEM((toks, rows, feats // toks), BF16),
        pltpu.VMEM((local, rows, token_feats), BF16),
        pltpu.VMEM((toks, local, rows, wide), BF16),
        pltpu.VMEM((toks, local, rows, wide), BF16),
        pltpu.VMEM((toks, local, rows, wide), BF16),
        pltpu.VMEM((local, slots, rows, dim), BF16),
        pltpu.VMEM((local, heads, dps, rows, dim), BF16),
        pltpu.VMEM((local, dps, rows, dim), BF16),
        pltpu.VMEM((local, dps - 1, rows, dim), BF16),
        pltpu.VMEM((local, dps - 1, rows, dim), BF16),
        pltpu.VMEM((rows, local, dim), F32),
        pltpu.VMEM((toks, block, dim), BF16),
        pltpu.VMEM((toks, block, dim), BF16),
        pltpu.VMEM((feats, feats), BF16),
        dma((3, local)), dma, dma((4, dps)), dma((slots, 2)),
        dma((toks,)), dma((toks,)), dma((toks,)), dma((toks,)),
        dma((toks, local // 2)), dma((toks, local // 2)),
        dma((local, dps)), dma((local, slots)), dma((local, dps)),
        dma((local,)), dma((local,)), dma((local, dps)), dma((local, dps)),
        dma((toks,)), dma((toks,)),
    ]
    gate_halves = gate_weight.reshape(2, -1, gate_weight.shape[1])
    return pl.pallas_call(
        functools.partial(fused_kernel, toks, dps, heads),
        out_shape=jax.ShapeDtypeStruct((1, split_rows, toks * local, dim), BF16),
        in_specs=[vmem] * 11 + [anywhere] * 4,
        out_specs=vmem,
        scratch_shapes=scratch,
        compiler_params=pltpu.CompilerParams(
            collective_id=0, has_side_effects=True, vmem_limit_bytes=63 * 2**20
        ),
    )(
        features, cross_down, cross_up, cross_bias.reshape(1, -1),
        feature_token.reshape(-1, 128), proj_bias, mix_gain, expand_bias, contract_bias,
        block_gain, gate_bias, gate_halves, proj_weight, expand_weight,
        contract_weight,
    )


def per_device(*arrays):
    features, gate_weight = arrays[0], arrays[13]
    toks = lax.axis_size("tok")
    local = arrays[5].shape[0]
    fits = (
        lax.axis_size("head") == 2
        and lax.axis_size("groups") == 2
        and lax.axis_size("dp") > 1
        and (DIM // toks) % 128 == 0
        and gate_weight.shape[1] % 128 == 0
        and features.shape[0] % 16 == 0
        and features.shape[0] % toks == 0
        and (features.shape[1] // toks) % 128 == 0
        and features.shape[0] // toks * local % 16 == 0
        and local % 8 == 0
    )
    return (fused_device if fits else plain_device)(*arrays)


def solution(mesh):
    placed = (
        P(("groups", "dp", "head"), "tok"),
        P("tok", None),
        P(None, "tok"),
        P("tok"),
        P("tok"),
        P("tok", None, None),
        P("tok", None),
        P("tok", None),
        P("tok", None, ("dp", "head")),
        P("tok", ("dp", "head")),
        P("tok", ("dp", "head"), None),
        P("tok", None),
        P("tok", None),
        P(None, ("dp", "head")),
        P(),
    )
    return jax.shard_map(
        per_device,
        mesh=mesh,
        in_specs=placed,
        out_specs=P(("groups", "dp", "head"), "tok", None, None),
        check_vma=False,
    )
```

```python
import functools

import jax
import jax.numpy as jnp
from jax import lax
from jax.experimental import pallas as pl
from jax.experimental.pallas import tpu as pltpu
from jax.sharding import PartitionSpec as P

FEAT_TOKENS = 32
DIM = 1536


def rms_norm(values, gain_row):
    scale = lax.rsqrt(jnp.mean(values * values, axis=-1, keepdims=True) + 1e-06)
    return values * scale * gain_row


def plain_device(
    features,
    cross_down,
    cross_up,
    cross_bias,
    feature_token,
    proj_weight,
    proj_bias,
    mix_gain,
    expand_weight,
    expand_bias,
    contract_weight,
    contract_bias,
    block_gain,
    gate_weight,
    gate_bias,
):
    rows_local = features.shape[0]
    local_tokens = proj_weight.shape[0]
    head_size = DIM // FEAT_TOKENS
    sources = lax.axis_size("tok")
    partial_low = jnp.dot(features, cross_down, preferred_element_type=jnp.float32)
    low_rank = lax.psum(partial_low.astype(jnp.bfloat16), "tok")
    lifted = jnp.dot(low_rank, cross_up, preferred_element_type=jnp.float32)
    widened = features.astype(jnp.float32)
    crossed = (widened * (lifted + cross_bias) + widened).astype(jnp.bfloat16)
    ordering = jnp.argsort(feature_token, stable=True)
    grouped = jnp.take(crossed, ordering, axis=1)
    routed = lax.all_to_all(grouped, "tok", split_axis=1, concat_axis=1, tiled=True)
    picked = (
        routed.reshape(rows_local, sources, local_tokens, -1)
        .transpose(0, 2, 1, 3)
        .reshape(rows_local, local_tokens, -1)
    )
    embedded = (
        jnp.einsum("rjf,jfd->rjd", picked, proj_weight, preferred_element_type=jnp.float32)
        + proj_bias
    )
    embedded = embedded.astype(jnp.bfloat16)
    heads_in = lax.all_to_all(embedded, "tok", split_axis=2, concat_axis=1, tiled=True)
    mixed_heads = (
        heads_in.reshape(rows_local, FEAT_TOKENS, local_tokens, head_size)
        .transpose(0, 2, 1, 3)
        .reshape(rows_local, local_tokens, DIM)
    )
    first_norm = rms_norm(
        mixed_heads.astype(jnp.float32) + embedded.astype(jnp.float32), mix_gain
    ).astype(jnp.bfloat16)
    every_row = lax.all_gather(first_norm, ("dp", "head"), axis=0, tiled=True)
    gelu_in = (
        jnp.einsum("rjd,jdh->rjh", every_row, expand_weight, preferred_element_type=jnp.float32)
        + expand_bias
    )
    activated = jax.nn.gelu(gelu_in).astype(jnp.bfloat16)
    summed = lax.psum_scatter(
        jnp.einsum(
            "rjh,jhd->rjd", activated, contract_weight, preferred_element_type=jnp.float32
        ).astype(jnp.bfloat16),
        ("dp", "head"),
        scatter_dimension=0,
        tiled=True,
    ).astype(jnp.float32)
    second_norm = rms_norm(
        summed + contract_bias + first_norm.astype(jnp.float32), block_gain
    ).astype(jnp.bfloat16)
    owned_rows = lax.all_to_all(second_norm, "tok", split_axis=0, concat_axis=1, tiled=True)
    flattened = owned_rows.reshape(-1, DIM)
    weight_piece = lax.all_gather(gate_weight, ("dp", "head"), axis=1, tiled=True)
    col_count = weight_piece.shape[1]
    logits = jnp.dot(flattened, weight_piece, preferred_element_type=jnp.float32).reshape(
        owned_rows.shape[0], owned_rows.shape[1], col_count
    )
    kept_cols = owned_rows.astype(jnp.float32)
    result = (kept_cols * jax.nn.sigmoid(logits + gate_bias)).astype(jnp.bfloat16)
    return result[None]


MESH = pl.DeviceIdType.MESH
F32 = jnp.float32
BF16 = jnp.bfloat16


def remote(src, dst, send_sem, recv_sem, device):
    return pltpu.make_async_remote_copy(
        src_ref=src, dst_ref=dst, send_sem=send_sem, recv_sem=recv_sem,
        device_id=device, device_id_type=MESH,
    )


def arrived(slot, send_sem, recv_sem, device):
    remote(slot, slot, send_sem, recv_sem, device).wait_recv()


def fused_kernel(
    toks, dps, heads,
    feat, cdown, cup, cbias, ftok, pbias, mgain, ebias, cbias2, bgain, gbias,
    gate_hbm, proj_hbm, exp_hbm, con_hbm,
    out,
    proj_v, exp_v, con_v, gate_v,
    low_buf, route_send, route_buf, picked, emb, head_buf, mixed, rows_v,
    part, sib_buf, xs_send, xs_buf, norm_rows, norm_send, norm_buf, perm, result,
    w_sem, gate_sem, gate_send, gate_recv, low_send, low_recv, rt_send, rt_recv,
    hd_send, hd_recv, ag_send, ag_recv, fw_send, sib_send, sib_recv, x_send, x_recv,
    nm_send, nm_recv,
):
    t = lax.axis_index("tok")
    p = lax.axis_index("dp")
    h = lax.axis_index("head")
    u = lax.axis_index("groups")
    mine = p * heads + h
    here = h * dps + p
    local_tokens, _, dim = proj_v.shape
    rows_local = feat.shape[0]
    feats_local = feat.shape[1]
    wide = dim // toks
    total_tokens = toks * local_tokens
    head_size = dim // total_tokens
    sibling = {"head": 1 - h}
    replica = {"groups": 1 - u}

    def tok_at(q):
        return lax.rem(t + q, toks)

    def dp_at(q):
        return lax.rem(p + q, dps)

    def proj_copy(j):
        return pltpu.make_async_copy(proj_hbm.at[j], proj_v.at[j], w_sem.at[0, j])

    def exp_copy(j):
        return pltpu.make_async_copy(exp_hbm.at[j], exp_v.at[j], w_sem.at[1, j])

    def con_copy(j):
        return pltpu.make_async_copy(con_hbm.at[j], con_v.at[j], w_sem.at[2, j])

    gate_own = pltpu.make_async_copy(gate_hbm, gate_v.at[mine], gate_sem)
    gate_own.start()
    for j in range(local_tokens):
        proj_copy(j).start()

    barrier = pltpu.get_barrier_semaphore()
    for q in range(1, toks):
        pl.semaphore_signal(barrier, inc=1, device_id={"tok": tok_at(q)}, device_id_type=MESH)
    for q in range(1, dps):
        pl.semaphore_signal(barrier, inc=1, device_id={"dp": dp_at(q)}, device_id_type=MESH)
    pl.semaphore_signal(barrier, inc=1, device_id=sibling, device_id_type=MESH)
    pl.semaphore_signal(barrier, inc=1, device_id=replica, device_id_type=MESH)

    low_buf[t] = jnp.dot(feat[...], cdown[...], preferred_element_type=F32)
    pl.semaphore_wait(barrier, toks - 1 + dps - 1 + 2)

    def low_copy(q):
        return remote(low_buf.at[t], low_buf.at[t], low_send.at[q], low_recv.at[t], {"tok": tok_at(q)})

    for q in range(1, toks):
        low_copy(q).start()

    gate_own.wait()

    def gate_copy(q):
        if q == 0:
            slot = gate_v.at[mine]
            return remote(slot, slot, gate_send.at[0, q], gate_recv.at[mine, 0], sibling)
        slot = gate_v.at[mine, u]
        return remote(slot, slot, gate_send.at[0, q], gate_recv.at[mine, u], {"dp": dp_at(q)})

    def gate_forward(q, kind):
        source = dp_at(q) * heads + h
        half = 1 - u if kind == 3 else u
        device = replica if kind == 1 else sibling
        slot = gate_v.at[source, half]
        return remote(slot, slot, gate_send.at[kind, q], gate_recv.at[source, half], device)

    def gate_arrived(source, half):
        arrived(gate_v.at[source, half], gate_send.at[0, 0], gate_recv.at[source, half], sibling)

    for q in range(dps):
        gate_copy(q).start()

    lanes = 128
    share = feats_local // total_tokens
    feature_at = lax.broadcasted_iota(jnp.int32, (lanes, lanes), 0)
    feature_of = lax.broadcasted_iota(jnp.int32, (lanes, lanes), 1)
    place_at = lax.broadcasted_iota(jnp.int32, (feats_local, lanes), 0)
    per_block = lanes // total_tokens
    for b in range(feats_local // lanes):
        token_row = ftok[b : b + 1, :]
        across = jnp.broadcast_to(token_row, (lanes, lanes))
        along = across.astype(F32).T.astype(jnp.int32)
        earlier = jnp.logical_and(across == along, feature_at < feature_of)
        rank = jnp.sum(jnp.where(earlier, 1.0, 0.0), axis=0, keepdims=True).astype(jnp.int32)
        place = token_row * share + b * per_block + rank
        perm[:, b * lanes : (b + 1) * lanes] = jnp.where(place_at == place, 1.0, 0.0).astype(BF16)

    for q in range(1, toks):
        source = tok_at(q)
        arrived(low_buf.at[source], low_send.at[q], low_recv.at[source], {"tok": source})
    low = low_buf[0]
    for s in range(1, toks):
        low = low + low_buf[s]
    lifted = jnp.dot(low.astype(BF16), cup[...], preferred_element_type=F32)
    widened = feat[...].astype(F32)
    crossed = (widened * (lifted + cbias[...]) + widened).astype(BF16)
    grouped = lax.dot_general(
        crossed, perm[...], (((1,), (1,)), ((), ())), preferred_element_type=F32
    ).astype(BF16)
    span = feats_local // toks
    for s in range(toks):
        route_send[s] = grouped[:, s * span : (s + 1) * span]

    def route_copy(q):
        target = tok_at(q)
        return remote(route_send.at[target], route_buf.at[t], rt_send.at[q], rt_recv.at[t], {"tok": target})

    for q in range(1, toks):
        route_copy(q).start()
    route_buf[t] = route_send[t]
    for j in range(local_tokens):
        exp_copy(j).start()
        con_copy(j).start()
    for q in range(1, toks):
        source = tok_at(q)
        arrived(route_buf.at[source], rt_send.at[q], rt_recv.at[source], {"tok": source})
    for s in range(toks):
        for j in range(local_tokens):
            picked[j, :, s * share : (s + 1) * share] = route_buf[s, :, j * share : (j + 1) * share]

    def embed(j, carry):
        proj_copy(j).wait()
        value = jnp.dot(picked[j], proj_v[j], preferred_element_type=F32) + pbias[pl.ds(j, 1), :]
        value = value.astype(BF16)
        for s in range(toks):
            emb[s, j] = value[:, s * wide : (s + 1) * wide]
        return carry

    lax.fori_loop(0, local_tokens, embed, 0)

    chunk = 2
    chunks = local_tokens // chunk

    def head_copy(q, c):
        target = tok_at(q)
        cut = pl.ds(c * chunk, chunk)
        return remote(
            head_buf.at[target, cut], mixed.at[t, cut], hd_send.at[q, c], hd_recv.at[t, c], {"tok": target}
        )

    for c in range(chunks):

        def turn(target, carry):
            for k in range(c * chunk, (c + 1) * chunk):
                for i in range(local_tokens):
                    head_buf[target, k, :, i * head_size : (i + 1) * head_size] = emb[
                        target, i, :, k * head_size : (k + 1) * head_size
                    ]
            return carry

        lax.fori_loop(0, toks, turn, 0)
        for q in range(1, toks):
            head_copy(q, c).start()
    mixed[t] = head_buf[t]

    for q in range(1, dps):
        gate_arrived(dp_at(q) * heads + h, u)
        gate_forward(q, 1).start()
        gate_forward(q, 2).start()

    def gather_copy(j, q):
        slot = rows_v.at[j, here]
        device = sibling if q == 0 else {"dp": dp_at(q)}
        return remote(slot, slot, ag_send.at[j, q], ag_recv.at[j, here], device)

    def gather_forward(j, q):
        source = h * dps + dp_at(q)
        slot = rows_v.at[j, source]
        return remote(slot, slot, fw_send.at[j, q], ag_recv.at[j, source], sibling)

    def first(j, carry):
        sums = []
        square = jnp.zeros((rows_local, 1), F32)
        for s in range(toks):
            value = mixed[s, j].astype(F32) + emb[s, j].astype(F32)
            sums.append(value)
            square = square + jnp.sum(value * value, axis=1, keepdims=True)
        scale = lax.rsqrt(square * (1.0 / dim) + 1e-06)
        for s in range(toks):
            gain = mgain[pl.ds(j, 1), s * wide : (s + 1) * wide]
            rows_v[j, here, :, s * wide : (s + 1) * wide] = (sums[s] * scale * gain).astype(BF16)
        for q in range(dps):
            gather_copy(j, q).start()
        return carry

    for c in range(chunks):
        for q in range(1, toks):
            source = tok_at(q)
            slot = mixed.at[source, pl.ds(c * chunk, chunk)]
            arrived(slot, hd_send.at[q, c], hd_recv.at[source, c], {"tok": source})
        lax.fori_loop(c * chunk, (c + 1) * chunk, first, 0)

    def forward(j):
        for q in range(1, dps):
            source = h * dps + dp_at(q)
            arrived(rows_v.at[j, source], fw_send.at[j, q], ag_recv.at[j, source], sibling)
            gather_forward(j, q).start()

    def pair_copy(j):
        return remote(part.at[j, 1 - h], sib_buf.at[j], sib_send.at[j], sib_recv.at[j], sibling)

    def network(j):
        for q in range(dps):
            source = (1 - h) * dps + dp_at(q)
            arrived(rows_v.at[j, source], fw_send.at[j, q], ag_recv.at[j, source], sibling)
        exp_copy(j).wait()
        con_copy(j).wait()
        everything = rows_v[j].reshape(heads * dps * rows_local, dim)
        inner = jnp.dot(everything, exp_v[j], preferred_element_type=F32) + ebias[pl.ds(j, 1), :]
        active = jax.nn.gelu(inner).astype(BF16)
        sums = jnp.dot(active, con_v[j], preferred_element_type=F32).astype(BF16)
        part[j] = sums.reshape(heads, dps, rows_local, dim)
        pair_copy(j).start()

    def cross_copy(j, q):
        return remote(
            xs_send.at[j, q - 1], xs_buf.at[j, q - 1], x_send.at[j, q], x_recv.at[j, q], {"dp": dp_at(q)}
        )

    def combine(j):
        arrived(sib_buf.at[j], sib_send.at[j], sib_recv.at[j], sibling)
        for q in range(1, dps):
            target = dp_at(q)
            both = part[j, h, target].astype(F32) + sib_buf[j, target].astype(F32)
            xs_send[j, q - 1] = both.astype(BF16)
            cross_copy(j, q).start()

    split_rows = rows_local // toks
    group = norm_buf.shape[2] // split_rows
    groups_local = local_tokens // group

    def norm_copy(q, k):
        target = tok_at(q)
        return remote(
            norm_send.at[target, k], norm_buf.at[t, k], nm_send.at[q, k], nm_recv.at[t, k], {"tok": target}
        )

    def leave(k):
        for s in range(toks):
            norm_send[s, k] = norm_rows[k, s].astype(BF16)
        for q in range(1, toks):
            norm_copy(q, k).start()
        norm_buf[t, k] = norm_send[t, k]

    def finish(j):
        total = part[j, h, p].astype(F32) + sib_buf[j, p].astype(F32)
        for q in range(1, dps):
            arrived(xs_buf.at[j, q - 1], x_send.at[j, q], x_recv.at[j, q], sibling)
            total = total + xs_buf[j, q - 1].astype(F32)
        total = total + cbias2[pl.ds(j, 1), :] + rows_v[j, here].astype(F32)
        scale = lax.rsqrt(jnp.sum(total * total, axis=1, keepdims=True) * (1.0 / dim) + 1e-06)
        value = total * scale * bgain[pl.ds(j, 1), :]
        for r in range(rows_local):
            place = (r % split_rows) * group + j % group
            norm_rows[j // group, r // split_rows, pl.ds(place, 1), :] = value[r : r + 1, :]

    def step(i, carry):
        @pl.when(i < local_tokens)
        def _():
            forward(i)

        @pl.when(jnp.logical_and(i >= 1, i < local_tokens + 1))
        def _():
            network(i - 1)

        @pl.when(jnp.logical_and(i >= 2, i < local_tokens + 2))
        def _():
            combine(i - 2)

        @pl.when(i >= 4)
        def _():
            finish(i - 4)

        for k in range(groups_local):

            @pl.when(i == 3 + group * (k + 1))
            def _():
                leave(k)

        return carry

    lax.fori_loop(0, local_tokens + 4, step, 0)

    for q in range(1, dps):
        gate_arrived(dp_at(q) * heads + h, 1 - u)
        gate_forward(q, 3).start()

    beside = gate_v.at[p * heads + (1 - h)]
    arrived(beside, gate_send.at[0, 0], gate_recv.at[p * heads + (1 - h), 0], sibling)
    for q in range(1, dps):
        for half in range(2):
            gate_arrived(dp_at(q) * heads + (1 - h), half)
    for q in range(1, toks):
        source = tok_at(q)
        for k in range(groups_local):
            arrived(norm_buf.at[source, k], nm_send.at[q, k], nm_recv.at[source, k], {"tok": source})

    gate_row = gbias[...].reshape(1, dim)
    block = group * split_rows
    count = toks * groups_local
    states = norm_buf[...].reshape(count * block, dim)
    columns = gate_v.shape[3]
    for c in range(dps * heads):
        cut = slice(c * columns, (c + 1) * columns)
        logits = jnp.dot(states, gate_v[c].reshape(dim, columns), preferred_element_type=F32) + gate_row[:, cut]
        kept = norm_buf[:, :, :, cut].reshape(count * block, columns).astype(F32)
        gated = kept * jax.nn.sigmoid(logits)
        for b in range(count):
            for r in range(split_rows):
                first_row = b * block + r * group
                result[r, b * group : (b + 1) * group, :] = gated[first_row : first_row + group, :]
        for r in range(split_rows):
            out[0, r, :, cut] = result[r].astype(BF16)

    for q in range(1, toks):
        low_copy(q).wait_send()
        route_copy(q).wait_send()
        for c in range(chunks):
            head_copy(q, c).wait_send()
        for k in range(groups_local):
            norm_copy(q, k).wait_send()
    for q in range(dps):
        gate_copy(q).wait_send()
    for q in range(1, dps):
        for kind in range(1, 4):
            gate_forward(q, kind).wait_send()

    def drain(j, carry):
        for q in range(dps):
            gather_copy(j, q).wait_send()
        for q in range(1, dps):
            gather_forward(j, q).wait_send()
            cross_copy(j, q).wait_send()
        pair_copy(j).wait_send()
        return carry

    lax.fori_loop(0, local_tokens, drain, 0)


def fused_device(
    features, cross_down, cross_up, cross_bias, feature_token, proj_weight, proj_bias,
    mix_gain, expand_weight, expand_bias, contract_weight, contract_bias, block_gain,
    gate_weight, gate_bias,
):
    toks, dps, heads = lax.axis_size("tok"), lax.axis_size("dp"), lax.axis_size("head")
    rows, feats = features.shape
    local, token_feats, dim = proj_weight.shape
    hidden = expand_weight.shape[2]
    wide = dim // toks
    split_rows = rows // toks
    halves = split_rows * local // 16
    vmem = pl.BlockSpec(memory_space=pltpu.VMEM)
    anywhere = pl.BlockSpec(memory_space=pl.ANY)
    dma = pltpu.SemaphoreType.DMA
    slots = heads * dps
    scratch = [
        pltpu.VMEM((local, token_feats, dim), BF16),
        pltpu.VMEM((local, dim, hidden), BF16),
        pltpu.VMEM((local, hidden, dim), BF16),
        pltpu.VMEM((slots, 2, dim // 2, gate_weight.shape[1]), BF16),
        pltpu.VMEM((toks, rows, cross_down.shape[1]), F32),
        pltpu.VMEM((toks, rows, feats // toks), BF16),
        pltpu.VMEM((toks, rows, feats // toks), BF16),
        pltpu.VMEM((local, rows, token_feats), BF16),
        pltpu.VMEM((toks, local, rows, wide), BF16),
        pltpu.VMEM((toks, local, rows, wide), BF16),
        pltpu.VMEM((toks, local, rows, wide), BF16),
        pltpu.VMEM((local, slots, rows, dim), BF16),
        pltpu.VMEM((local, heads, dps, rows, dim), BF16),
        pltpu.VMEM((local, dps, rows, dim), BF16),
        pltpu.VMEM((local, dps - 1, rows, dim), BF16),
        pltpu.VMEM((local, dps - 1, rows, dim), BF16),
        pltpu.VMEM((halves, toks, 16, dim), F32),
        pltpu.VMEM((toks, halves, 16, dim), BF16),
        pltpu.VMEM((toks, halves, 16, dim), BF16),
        pltpu.VMEM((feats, feats), BF16),
        pltpu.VMEM((split_rows, toks * local, gate_weight.shape[1]), F32),
        dma((3, local)), dma, dma((4, dps)), dma((slots, 2)),
        dma((toks,)), dma((toks,)), dma((toks,)), dma((toks,)),
        dma((toks, local // 2)), dma((toks, local // 2)),
        dma((local, dps)), dma((local, slots)), dma((local, dps)),
        dma((local,)), dma((local,)), dma((local, dps)), dma((local, dps)),
        dma((toks, halves)), dma((toks, halves)),
    ]
    gate_halves = gate_weight.reshape(2, -1, gate_weight.shape[1])
    return pl.pallas_call(
        functools.partial(fused_kernel, toks, dps, heads),
        out_shape=jax.ShapeDtypeStruct((1, split_rows, toks * local, dim), BF16),
        in_specs=[vmem] * 11 + [anywhere] * 4,
        out_specs=vmem,
        scratch_shapes=scratch,
        compiler_params=pltpu.CompilerParams(
            collective_id=0, has_side_effects=True, vmem_limit_bytes=63 * 2**20
        ),
    )(
        features, cross_down, cross_up, cross_bias.reshape(1, -1),
        feature_token.reshape(-1, 128), proj_bias, mix_gain, expand_bias, contract_bias,
        block_gain, gate_bias, gate_halves, proj_weight, expand_weight,
        contract_weight,
    )


def per_device(*arrays):
    features, gate_weight = arrays[0], arrays[13]
    toks = lax.axis_size("tok")
    local = arrays[5].shape[0]
    fits = (
        lax.axis_size("head") == 2
        and lax.axis_size("groups") == 2
        and lax.axis_size("dp") > 1
        and (DIM // toks) % 128 == 0
        and gate_weight.shape[1] % 128 == 0
        and features.shape[0] % 16 == 0
        and features.shape[0] % toks == 0
        and (features.shape[1] // toks) % 128 == 0
        and features.shape[0] // toks * local % 16 == 0
        and local % 8 == 0
        and 16 % (features.shape[0] // toks) == 0
    )
    return (fused_device if fits else plain_device)(*arrays)


def solution(mesh):
    placed = (
        P(("groups", "dp", "head"), "tok"),
        P("tok", None),
        P(None, "tok"),
        P("tok"),
        P("tok"),
        P("tok", None, None),
        P("tok", None),
        P("tok", None),
        P("tok", None, ("dp", "head")),
        P("tok", ("dp", "head")),
        P("tok", ("dp", "head"), None),
        P("tok", None),
        P("tok", None),
        P(None, ("dp", "head")),
        P(),
    )
    return jax.shard_map(
        per_device,
        mesh=mesh,
        in_specs=placed,
        out_specs=P(("groups", "dp", "head"), "tok", None, None),
        check_vma=False,
    )
```
